512 devices in a mesh: blk: 128 (over z, x, y_hi), head: 4 (over y_lo, core).
Axes of the slice: x: 4, y: 4 (y_hi: 2, y_lo: 2; y = y_hi * 2 + y_lo), z: 16, core: 2. Of those that a mesh axis runs over, the one named last changes fastest.
Arguments:
- vertices: bfloat16 [16384, 1024], P('blk'), may hold values from -6 to 6
- grad_out: bfloat16 [16384, 1024], P('blk'), may hold values from -6 to 6
- w_query: bfloat16 [1024, 1024], P(None, 'head'), may hold values from -0.1875 to 0.1875
- w_key: bfloat16 [1024, 1024], P(None, 'head'), may hold values from -0.1875 to 0.1875
- w_value: bfloat16 [1024, 1024], P(None, 'head'), may hold values from -0.1875 to 0.1875
- w_out: bfloat16 [1024, 1024], P('head'), may hold values from -0.1875 to 0.1875
- pair_bins: int32 [512, 20], P('blk'), may hold values from 0 to 31
- bias_table: float32 [4, 32], replicated, may hold values from -4 to 310
- head_index: int32 [16], P('head'), may hold values from 0 to 3
Outputs:
- grad_vertices: bfloat16 [16384, 1024], P('blk', 'head')
The draws below stay inside these ranges and needn't reach their ends.
All inputs are finite; a program needn't handle non-finite values.
Results may differ from the reference program's by a relative error of at most 0.017.
Values may be sent and summed in bfloat16 or wider, within the bound.
A program may use at most 64 MiB of HBM per device.

```python
import jax
import jax.numpy as jnp
from jax import lax

D = 1024
HEADS = 16
HEAD_DIM = 64
VTX_DEV = 128
REACH = 2
GROUP = 32
NBINS = 32
TABLES = 4
VERTS = 16384


def draw_bias_table(key, part):
    key = jax.random.fold_in(key, 7)
    return jnp.clip(1.5 * jax.random.normal(key, (TABLES, NBINS), jnp.float32), -4.0, 4.0)


def place_ends(values, own_key, smallest, top_value):
    dims = values.shape
    spot = [jax.random.randint(jax.random.fold_in(own_key, axis), (), 0, dims[axis]) for axis in range(len(dims))]
    values = values.at[tuple(spot)].set(smallest)
    longest = dims.index(max(dims))
    spot[longest] = (spot[longest] + 1) % dims[longest]
    return values.at[tuple(spot)].set(top_value)


def block_scale(own_key, dims, shards, least, high):
    factor_of, own = 1.0, jax.random.fold_in(own_key, 6)
    for position, shards_of in shards:
        heights = jnp.exp(jax.random.uniform(jax.random.fold_in(own, position), (shards_of,), jnp.float32, least / len(shards), high / len(shards)))
        factor_of = factor_of * jnp.repeat(heights, dims[position] // shards_of).reshape([-1 if axis == position else 1 for axis in range(len(dims))])
    return factor_of


def normal_values(own_key, extent, deviation, reach, cuts=(), held_as=jnp.bfloat16):
    result = jax.random.normal(own_key, extent, jnp.float32) * deviation
    if len(cuts) > 0:
        result = block_scale(own_key, extent, cuts, -0.22, 0.18) * result
    return jnp.clip(result, min=-reach, max=reach).astype(held_as)


def setup_inputs(seed: int = 0) -> dict:
    arg_keys = jax.random.split(jax.random.key(seed), 10)
    return {
        "vertices": normal_values(arg_keys[0], (VERTS, D), 1.0, 6.0, ((0, 128),)),
        "grad_out": normal_values(arg_keys[1], (VERTS, D), 1.0, 6.0, ((0, 128),)),
        "w_query": normal_values(arg_keys[2], (D, D), D ** -0.5, 0.1875, ((1, 4),)),
        "w_key": normal_values(arg_keys[3], (D, D), D ** -0.5, 0.1875, ((1, 4),)),
        "w_value": normal_values(arg_keys[4], (D, D), D ** -0.5, 0.1875, ((1, 4),)),
        "w_out": normal_values(arg_keys[5], (D, D), D ** -0.5, 0.1875, ((0, 4),)),
        "pair_bins": place_ends(jax.random.randint(arg_keys[6], (VERTS // GROUP, (2 * REACH + 1) * (VTX_DEV // GROUP)), 0, NBINS), jax.random.fold_in(arg_keys[6], 1), 0, NBINS - 1).astype(jnp.int32),
        "bias_table": draw_bias_table(jax.random.fold_in(arg_keys[9], 71), 0),
        "head_index": place_ends(jax.random.randint(arg_keys[8], (HEADS,), 0, TABLES), jax.random.fold_in(arg_keys[8], 1), 0, TABLES - 1).astype(jnp.int32),
    }


def spread_bias(group_bias):
    count, rows_g, cols_g = group_bias.shape
    wide = jnp.broadcast_to(group_bias[:, :, None, :, None], (count, rows_g, GROUP, cols_g, GROUP))
    return wide.reshape(count, rows_g * GROUP, cols_g * GROUP)


def reference(vertices, grad_out, w_query, w_key, w_value, w_out, pair_bins, bias_table, head_index):
    block_count = VERTS // VTX_DEV
    width_blocks = 2 * REACH + 1
    score_scale = HEAD_DIM ** -0.5
    queries = jnp.dot(vertices, w_query, preferred_element_type=jnp.float32).astype(jnp.bfloat16)
    keys_all = jnp.dot(vertices, w_key, preferred_element_type=jnp.float32).astype(jnp.bfloat16)
    values_all = jnp.dot(vertices, w_value, preferred_element_type=jnp.float32).astype(jnp.bfloat16)
    grad_attn = jnp.dot(grad_out, w_out.T, preferred_element_type=jnp.float32).astype(jnp.bfloat16)
    head_table = bias_table[head_index]

    def as_blocks(array):
        return array.reshape(block_count, VTX_DEV, HEADS, HEAD_DIM)

    query_blk = as_blocks(queries)
    key_blk = as_blocks(keys_all)
    value_blk = as_blocks(values_all)
    grad_blk = as_blocks(grad_attn)
    bin_blocks = pair_bins.reshape(block_count, VTX_DEV // GROUP, width_blocks * (VTX_DEV // GROUP))

    def window_ids(block_id):
        return ((block_id + jnp.arange(-REACH, REACH + 1, dtype=jnp.int32)) % block_count).astype(jnp.int32)

    def one_block(block_id):
        block_ids = window_ids(block_id)
        query_f = query_blk[block_id].astype(jnp.float32)
        grad_f = grad_blk[block_id].astype(jnp.float32)
        key_f = key_blk[block_ids].reshape(width_blocks * VTX_DEV, HEADS, HEAD_DIM).astype(jnp.float32)
        value_f = value_blk[block_ids].reshape(width_blocks * VTX_DEV, HEADS, HEAD_DIM).astype(jnp.float32)
        bias = spread_bias(head_table[:, bin_blocks[block_id]])
        scores = jnp.einsum('qhd,khd->hqk', query_f, key_f) * score_scale + bias
        row_peak = jnp.max(scores, axis=2, keepdims=True)
        expo = jnp.exp(scores - row_peak)
        attend = expo / jnp.sum(expo, axis=2, keepdims=True)
        attend_low = attend.astype(jnp.bfloat16).astype(jnp.float32)
        output = jnp.einsum('hqk,khd->qhd', attend_low, value_f).astype(jnp.bfloat16)
        row_dot = jnp.sum(grad_f * output.astype(jnp.float32), axis=2)
        grad_weights = jnp.einsum('qhd,khd->hqk', grad_f, value_f)
        grad_scores = (attend * (grad_weights - row_dot.T[:, :, None])).astype(jnp.bfloat16).astype(jnp.float32)
        grad_query = (jnp.einsum('hqk,khd->qhd', grad_scores, key_f) * score_scale).astype(jnp.bfloat16)
        grad_key = jnp.einsum('hqk,qhd->khd', grad_scores, query_f) * score_scale
        grad_value = jnp.einsum('hqk,qhd->khd', attend_low, grad_f)
        return grad_query, grad_key, grad_value

    def advance(carry, block_id):
        key_acc, value_acc = carry
        grad_query, grad_key, grad_value = one_block(block_id)
        block_ids = window_ids(block_id)
        key_acc = key_acc.at[block_ids].add(grad_key.reshape(width_blocks, VTX_DEV, HEADS, HEAD_DIM))
        value_acc = value_acc.at[block_ids].add(grad_value.reshape(width_blocks, VTX_DEV, HEADS, HEAD_DIM))
        return (key_acc, value_acc), grad_query

    zeros_acc = jnp.zeros((block_count, VTX_DEV, HEADS, HEAD_DIM), jnp.float32)
    (key_acc, value_acc), query_grads = lax.scan(advance, (zeros_acc, zeros_acc), jnp.arange(block_count, dtype=jnp.int32))
    grad_query = query_grads.reshape(VERTS, D)
    grad_key = key_acc.reshape(VERTS, D).astype(jnp.bfloat16)
    grad_value = value_acc.reshape(VERTS, D).astype(jnp.bfloat16)
    total = jnp.dot(grad_query, w_query.T, preferred_element_type=jnp.float32)
    total = total + jnp.dot(grad_key, w_key.T, preferred_element_type=jnp.float32)
    total = total + jnp.dot(grad_value, w_value.T, preferred_element_type=jnp.float32)
    return total.astype(jnp.bfloat16)
```

```python
import functools
import math

import jax
import jax.numpy as jnp
from jax import lax
from jax.experimental import pallas as pl
from jax.experimental.pallas import tpu as pltpu
from jax.sharding import PartitionSpec as P

HEAD_DIM = 64
REACH = 2
GROUP = 32
WIDTH = 2 * REACH + 1
PAIR = 2 * HEAD_DIM
LOG2E = math.log2(math.e)
MESH = pl.DeviceIdType.MESH
F32 = jnp.float32
BF16 = jnp.bfloat16
NEAR = (1, -1, 2, -2)


def dot_nn(a, b):
    return lax.dot_general(a, b, (((1,), (0,)), ((), ())), preferred_element_type=F32)


def dot_nt(a, b):
    return lax.dot_general(a, b, (((1,), (1,)), ((), ())), preferred_element_type=F32)


def kernel(
    nb,
    x_hbm, g_hbm, wq_hbm, wk_hbm, wv_hbm, wo_hbm, bins_hbm, table_hbm, hid_hbm,
    out_ref,
    x, g, wq, wk, wv, wo, bins, table, hid,
    kv, qg, qbd, gbd, ew, dp, s2, dp2, bias, st_src, st_in, dk, dv, part, red_src, red_in,
    in_sem, kv_send, kv_recv, qg_send, qg_recv, st_send, st_recv, red_send, red_recv,
):
    rows = x.shape[0]
    feats = wq.shape[1]
    pairs = feats // PAIR
    groups = rows // GROUP
    me = lax.axis_index("blk")
    head = lax.axis_index("head")
    peers = (lax.rem(head + 2, 4), 3 - head, head + 1 - 2 * lax.rem(head, 2))

    loads = [
        pltpu.make_async_copy(src, dst, in_sem.at[i])
        for i, (src, dst) in enumerate(
            (
                (x_hbm, x), (wk_hbm, wk), (wv_hbm, wv), (wq_hbm, wq), (g_hbm, g), (wo_hbm, wo),
                (bins_hbm, bins), (table_hbm, table), (hid_hbm, hid),
            )
        )
    ]
    for load in loads:
        load.start()

    def block(by):
        return lax.rem(me + (by + nb), nb)

    barrier = pltpu.get_barrier_semaphore()
    for by in NEAR:
        pl.semaphore_signal(barrier, inc=1, device_id=(block(by), head), device_id_type=MESH)
    for peer in peers:
        pl.semaphore_signal(barrier, inc=1, device_id=(me, peer), device_id_type=MESH)

    def to_block(src, dst, send, recv, i):
        by = NEAR[i]
        return pltpu.make_async_remote_copy(
            src_ref=src,
            dst_ref=dst.at[REACH - by],
            send_sem=send.at[i],
            recv_sem=recv.at[REACH - by],
            device_id=(block(by), head),
            device_id_type=MESH,
        )

    def wait_from(copies, slot):
        copies[NEAR.index(REACH - slot)].wait_recv()

    loads[0].wait()
    loads[1].wait()
    kv[REACH, 0] = dot_nn(x[...], wk[...]).astype(BF16)
    loads[2].wait()
    kv[REACH, 1] = dot_nn(x[...], wv[...]).astype(BF16)
    pl.semaphore_wait(barrier, len(NEAR) + len(peers))
    kv_out = [to_block(kv.at[REACH], kv, kv_send, kv_recv, i) for i in range(len(NEAR))]
    for copy in kv_out:
        copy.start()
    loads[3].wait()
    qg[REACH, 0] = (dot_nn(x[...], wq[...]).astype(BF16).astype(F32) * (HEAD_DIM**-0.5)).astype(BF16)
    loads[4].wait()
    loads[5].wait()
    qg[REACH, 1] = dot_nt(g[...], wo[...]).astype(BF16)
    qg_out = [to_block(qg.at[REACH], qg, qg_send, qg_recv, i) for i in range(len(NEAR))]
    for copy in qg_out:
        copy.start()

    low_lane = lax.broadcasted_iota(jnp.int32, (rows, PAIR), 1) < HEAD_DIM
    zero = jnp.zeros((rows, PAIR), BF16)

    def spread(slot):
        for pr in range(pairs):
            cols = pl.ds(pr * PAIR, PAIR)
            for which, dst in ((0, qbd), (1, gbd)):
                both = qg[slot, which, :, cols]
                dst[slot, pr, pl.ds(0, rows), :] = jnp.where(low_lane, both, zero)
                dst[slot, pr, pl.ds(rows, rows), :] = jnp.where(low_lane, zero, both)

    spread(REACH)

    loads[6].wait()
    loads[7].wait()
    loads[8].wait()
    lane_group = lax.broadcasted_iota(jnp.int32, (1, rows), 1) // GROUP

    def bias_rows(slot, carry):
        for h in range(2 * pairs):
            lines = []
            for kg in range(groups):
                line = jnp.zeros((1, rows), F32)
                for gr in range(groups):
                    line = jnp.where(lane_group == gr, table[hid[h], bins[gr, slot * groups + kg]], line)
                lines.append(line)
            bias[slot, h // 2, :, pl.ds((h % 2) * rows, rows)] = jnp.concatenate(lines, axis=0) * LOG2E
        return carry

    lax.fori_loop(0, WIDTH, bias_rows, 0)

    def grouped(tile):
        return tile.reshape(groups, GROUP, 2 * rows)

    stats = {}

    def key_tile(slot):
        for pr in range(pairs):
            cols = pl.ds(pr * PAIR, PAIR)
            score = dot_nt(kv[slot, 0, :, cols], qbd[REACH, pr])
            weigh = dot_nt(kv[slot, 1, :, cols], gbd[REACH, pr])
            shift = bias[slot, pr]
            logit = grouped(score) * LOG2E + shift[:, None, :]
            peak = jnp.max(logit, axis=(0, 1), keepdims=True)
            expo = jnp.exp2(logit - peak).reshape(rows, 2 * rows)
            ew[slot, pr] = expo
            dp[slot, pr] = weigh
            total = jnp.sum(expo, axis=0, keepdims=True)
            cross = jnp.sum(expo * weigh, axis=0, keepdims=True)
            stats[slot, pr] = (peak.reshape(1, 2 * rows), total, cross)

    order = (REACH, 0, 2 * REACH, 1, 3)
    for slot in order:
        if slot != REACH:
            wait_from(kv_out, slot)
        key_tile(slot)

    scale = {}
    dots = []
    for pr in range(pairs):
        top = functools.reduce(jnp.maximum, [stats[s, pr][0] for s in range(WIDTH)])
        lift = [jnp.exp2(stats[s, pr][0] - top) for s in range(WIDTH)]
        total = sum(stats[s, pr][1] * lift[s] for s in range(WIDTH))
        cross = sum(stats[s, pr][2] * lift[s] for s in range(WIDTH))
        inverse = 1.0 / total
        lse = top + jnp.log2(total)
        row_dot = cross * inverse
        dots.append(row_dot)
        for s in range(WIDTH):
            scale[s, pr] = lift[s] * inverse
            if s != REACH:
                st_src[s, pr, pl.ds(0, groups), :] = bias[s, pr] - lse
                st_src[s, pr, pl.ds(groups, groups), :] = jnp.broadcast_to(row_dot, (groups, 2 * rows))
    st_out = [to_block(st_src.at[REACH + NEAR[i]], st_in, st_send, st_recv, i) for i in range(len(NEAR))]
    for copy in st_out:
        copy.start()

    low_row = lax.broadcasted_iota(jnp.int32, (PAIR, rows), 0) < HEAD_DIM
    grad_query = []
    for pr in range(pairs):
        cols = pl.ds(pr * PAIR, PAIR)
        acc = jnp.zeros((PAIR, rows), F32)
        for slot in order:
            prob = ew[slot, pr] * scale[slot, pr]
            grad_score = (prob * (dp[slot, pr] - dots[pr])).astype(BF16)
            key_t = kv[slot, 0, :, cols].astype(F32).T
            key_m = jnp.concatenate(
                [jnp.where(low_row, key_t, 0.0), jnp.where(low_row, 0.0, key_t)], axis=1
            ).astype(BF16)
            stacked = jnp.concatenate([grad_score[:, :rows], grad_score[:, rows:]], axis=0)
            acc = acc + dot_nn(key_m, stacked)
            if slot == REACH:
                dk[pr] = dot_nn(grad_score, qbd[slot, pr])
                dv[pr] = dot_nn(prob.astype(BF16), gbd[slot, pr])
        grad_query.append((acc * (HEAD_DIM**-0.5)).T.astype(BF16))
    query_all = jnp.concatenate(grad_query, axis=1)
    part[...] = dot_nt(query_all, wq[...])

    others = (0, 2 * REACH, 1, 3)
    for slot in others:
        wait_from(qg_out, slot)
        spread(slot)
        for pr in range(pairs):
            cols = pl.ds(pr * PAIR, PAIR)
            s2[slot, pr] = dot_nt(kv[REACH, 0, :, cols], qbd[slot, pr]) * LOG2E
            dp2[slot, pr] = dot_nt(kv[REACH, 1, :, cols], gbd[slot, pr])

    for slot in others:
        wait_from(st_out, slot)
        for pr in range(pairs):
            shift = st_in[slot, pr, pl.ds(0, groups), :]
            row_dot = st_in[slot, pr, pl.ds(groups, 1), :]
            prob = jnp.exp2(grouped(s2[slot, pr]) + shift[:, None, :]).reshape(rows, 2 * rows)
            grad_score = (prob * (dp2[slot, pr] - row_dot)).astype(BF16)
            dk[pr] += dot_nn(grad_score, qbd[slot, pr])
            dv[pr] += dot_nn(prob.astype(BF16), gbd[slot, pr])

    key_all = jnp.concatenate([dk[pr].astype(BF16) for pr in range(pairs)], axis=1)
    value_all = jnp.concatenate([dv[pr].astype(BF16) for pr in range(pairs)], axis=1)

    def share(j):
        lines = pl.ds(pl.multiple_of(j * feats, feats), feats)
        return (
            part[:, lines]
            + dot_nt(key_all, wk[lines, :])
            + dot_nt(value_all, wv[lines, :])
        )

    red_out = []
    for i, peer in enumerate(peers):
        red_src[i] = share(peer).astype(BF16)
        copy = pltpu.make_async_remote_copy(
            src_ref=red_src.at[i],
            dst_ref=red_in.at[i],
            send_sem=red_send.at[i],
            recv_sem=red_recv.at[i],
            device_id=(me, peer),
            device_id_type=MESH,
        )
        copy.start()
        red_out.append(copy)
    total = share(head)
    for i in (2, 0, 1):
        red_out[i].wait_recv()
        total = total + red_in[i].astype(F32)
    out_ref[...] = total.astype(out_ref.dtype)
    for copy in (*kv_out, *qg_out, *st_out, *red_out):
        copy.wait_send()


def solution(mesh):
    nb = mesh.shape["blk"]

    def body(vertices, grad_out, w_query, w_key, w_value, w_out, pair_bins, bias_table, head_index):
        rows, width = vertices.shape
        feats = w_query.shape[1]
        pairs = feats // PAIR
        vmem, smem, dma = pltpu.VMEM, pltpu.SMEM, pltpu.SemaphoreType.DMA
        scratch = [
            vmem((rows, width), BF16),
            vmem((rows, width), BF16),
            vmem((width, feats), BF16),
            vmem((width, feats), BF16),
            vmem((width, feats), BF16),
            vmem((feats, width), BF16),
            smem(pair_bins.shape, jnp.int32),
            smem(bias_table.shape, F32),
            smem(head_index.shape, jnp.int32),
            vmem((WIDTH, 2, rows, feats), BF16),
            vmem((WIDTH, 2, rows, feats), BF16),
            vmem((WIDTH, pairs, 2 * rows, PAIR), BF16),
            vmem((WIDTH, pairs, 2 * rows, PAIR), BF16),
            vmem((WIDTH, pairs, rows, 2 * rows), F32),
            vmem((WIDTH, pairs, rows, 2 * rows), F32),
            vmem((WIDTH, pairs, rows, 2 * rows), F32),
            vmem((WIDTH, pairs, rows, 2 * rows), F32),
            vmem((WIDTH, pairs, rows // GROUP, 2 * rows), F32),
            vmem((WIDTH, pairs, 8, 2 * rows), F32),
            vmem((WIDTH, pairs, 8, 2 * rows), F32),
            vmem((pairs, rows, PAIR), F32),
            vmem((pairs, rows, PAIR), F32),
            vmem((rows, width), F32),
            vmem((3, rows, feats), BF16),
            vmem((3, rows, feats), BF16),
            dma((9,)),
            dma((4,)), dma((WIDTH,)),
            dma((4,)), dma((WIDTH,)),
            dma((4,)), dma((WIDTH,)),
            dma((3,)), dma((3,)),
        ]
        return pl.pallas_call(
            functools.partial(kernel, nb),
            out_shape=jax.ShapeDtypeStruct((rows, feats), BF16),
            in_specs=[pl.BlockSpec(memory_space=pl.ANY)] * 9,
            out_specs=pl.BlockSpec(memory_space=pltpu.VMEM),
            scratch_shapes=scratch,
            compiler_params=pltpu.CompilerParams(
                collective_id=0, has_side_effects=True, vmem_limit_bytes=40 * 2**20
            ),
            name="attend_backward",
        )(vertices, grad_out, w_query, w_key, w_value, w_out, pair_bins, bias_table, head_index)

    in_specs = (
        P("blk", None),
        P("blk", None),
        P(None, "head"),
        P(None, "head"),
        P(None, "head"),
        P("head", None),
        P("blk", None),
        P(),
        P("head"),
    )
    return jax.shard_map(body, mesh=mesh, in_specs=in_specs, out_specs=P("blk", "head"), check_vma=False)
```

```python
import functools
import math

import jax
import jax.numpy as jnp
from jax import lax
from jax.experimental import pallas as pl
from jax.experimental.pallas import tpu as pltpu
from jax.sharding import PartitionSpec as P

HEAD_DIM = 64
REACH = 2
GROUP = 32
WIDTH = 2 * REACH + 1
PAIR = 2 * HEAD_DIM
LOG2E = math.log2(math.e)
MESH = pl.DeviceIdType.MESH
F32 = jnp.float32
BF16 = jnp.bfloat16
NEAR = (1, -1, 2, -2)


def dot_nn(a, b):
    return lax.dot_general(a, b, (((1,), (0,)), ((), ())), preferred_element_type=F32)


def dot_nt(a, b):
    return lax.dot_general(a, b, (((1,), (1,)), ((), ())), preferred_element_type=F32)


def kernel(
    nb,
    x_hbm, g_hbm, wq_hbm, wk_hbm, wv_hbm, wo_hbm, bins_hbm, table_hbm, hid_hbm,
    out_ref,
    x, g, wq, wk, wv, wo, bins, table, hid,
    kv, qg, qbd, gbd, ew, dp, s2, dp2, bias, st_src, st_in, dk, dv, part, red_src, red_in,
    in_sem, kv_send, kv_recv, qg_send, qg_recv, st_send, st_recv, red_send, red_recv,
):
    rows = x.shape[0]
    feats = wq.shape[1]
    pairs = feats // PAIR
    groups = rows // GROUP
    me = lax.axis_index("blk")
    head = lax.axis_index("head")
    peers = (lax.rem(head + 2, 4), 3 - head, head + 1 - 2 * lax.rem(head, 2))

    loads = [
        pltpu.make_async_copy(src, dst, in_sem.at[i])
        for i, (src, dst) in enumerate(
            (
                (x_hbm, x), (wk_hbm, wk), (wv_hbm, wv), (wq_hbm, wq), (g_hbm, g), (wo_hbm, wo),
                (bins_hbm, bins), (table_hbm, table), (hid_hbm, hid),
            )
        )
    ]
    for load in loads:
        load.start()

    def block(by):
        return lax.rem(me + (by + nb), nb)

    barrier = pltpu.get_barrier_semaphore()
    for by in NEAR:
        pl.semaphore_signal(barrier, inc=1, device_id=(block(by), head), device_id_type=MESH)
    for peer in peers:
        pl.semaphore_signal(barrier, inc=1, device_id=(me, peer), device_id_type=MESH)

    def to_block(src, dst, send, recv, i):
        by = NEAR[i]
        return pltpu.make_async_remote_copy(
            src_ref=src,
            dst_ref=dst.at[REACH - by],
            send_sem=send.at[i],
            recv_sem=recv.at[REACH - by],
            device_id=(block(by), head),
            device_id_type=MESH,
        )

    def wait_from(copies, slot):
        copies[NEAR.index(REACH - slot)].wait_recv()

    loads[0].wait()
    loads[1].wait()
    kv[REACH, 0] = dot_nn(x[...], wk[...]).astype(BF16)
    loads[2].wait()
    kv[REACH, 1] = dot_nn(x[...], wv[...]).astype(BF16)
    pl.semaphore_wait(barrier, len(NEAR) + len(peers))
    kv_out = [to_block(kv.at[REACH], kv, kv_send, kv_recv, i) for i in range(len(NEAR))]
    for copy in kv_out:
        copy.start()
    loads[3].wait()
    qg[REACH, 0] = (dot_nn(x[...], wq[...]).astype(BF16).astype(F32) * (HEAD_DIM**-0.5)).astype(BF16)
    loads[4].wait()
    loads[5].wait()
    qg[REACH, 1] = dot_nt(g[...], wo[...]).astype(BF16)
    qg_out = [to_block(qg.at[REACH], qg, qg_send, qg_recv, i) for i in range(len(NEAR))]
    for copy in qg_out:
        copy.start()

    low_lane = lax.broadcasted_iota(jnp.int32, (rows, PAIR), 1) < HEAD_DIM
    zero = jnp.zeros((rows, PAIR), BF16)

    def spread(slot):
        for pr in range(pairs):
            cols = pl.ds(pr * PAIR, PAIR)
            for which, dst in ((0, qbd), (1, gbd)):
                both = qg[slot, which, :, cols]
                dst[slot, pr, pl.ds(0, rows), :] = jnp.where(low_lane, both, zero)
                dst[slot, pr, pl.ds(rows, rows), :] = jnp.where(low_lane, zero, both)

    spread(REACH)

    loads[6].wait()
    loads[7].wait()
    loads[8].wait()
    lane_group = lax.broadcasted_iota(jnp.int32, (1, rows), 1) // GROUP

    def bias_rows(slot, carry):
        for h in range(2 * pairs):
            lines = []
            for kg in range(groups):
                line = jnp.zeros((1, rows), F32)
                for gr in range(groups):
                    line = jnp.where(lane_group == gr, table[hid[h], bins[gr, slot * groups + kg]], line)
                lines.append(line)
            bias[slot, h // 2, :, pl.ds((h % 2) * rows, rows)] = jnp.concatenate(lines, axis=0) * LOG2E
        return carry

    lax.fori_loop(0, WIDTH, bias_rows, 0)

    def grouped(tile):
        return tile.reshape(groups, GROUP, 2 * rows)

    stats = {}

    def key_tile(slot):
        for pr in range(pairs):
            cols = pl.ds(pr * PAIR, PAIR)
            score = dot_nt(kv[slot, 0, :, cols], qbd[REACH, pr])
            weigh = dot_nt(kv[slot, 1, :, cols], gbd[REACH, pr])
            shift = bias[slot, pr]
            logit = grouped(score) * LOG2E + shift[:, None, :]
            peak = jnp.max(logit, axis=(0, 1), keepdims=True)
            expo = jnp.exp2(logit - peak).reshape(rows, 2 * rows)
            ew[slot, pr] = expo
            dp[slot, pr] = weigh
            total = jnp.sum(expo, axis=0, keepdims=True)
            cross = jnp.sum(expo * weigh, axis=0, keepdims=True)
            stats[slot, pr] = (peak.reshape(1, 2 * rows), total, cross)

    order = (REACH, 0, 2 * REACH, 1, 3)
    key_tile(REACH)
    wait_from(kv_out, order[1])
    key_tile(order[1])
    wait_from(kv_out, order[2])
    key_tile(order[2])
    wait_from(kv_out, order[3])
    key_tile(order[3])
    wait_from(kv_out, order[4])
    key_tile(order[4])

    scale = {}
    dots = []
    for pr in range(pairs):
        top = functools.reduce(jnp.maximum, [stats[s, pr][0] for s in range(WIDTH)])
        lift = [jnp.exp2(stats[s, pr][0] - top) for s in range(WIDTH)]
        total = sum(stats[s, pr][1] * lift[s] for s in range(WIDTH))
        cross = sum(stats[s, pr][2] * lift[s] for s in range(WIDTH))
        inverse = 1.0 / total
        lse = top + jnp.log2(total)
        row_dot = cross * inverse
        dots.append(row_dot)
        for s in range(WIDTH):
            scale[s, pr] = lift[s] * inverse
            if s != REACH:
                st_src[s, pr, pl.ds(0, groups), :] = bias[s, pr] - lse
                st_src[s, pr, pl.ds(groups, groups), :] = jnp.broadcast_to(row_dot, (groups, 2 * rows))
    st_out = [to_block(st_src.at[REACH + NEAR[i]], st_in, st_send, st_recv, i) for i in range(len(NEAR))]
    for copy in st_out:
        copy.start()

    low_row = lax.broadcasted_iota(jnp.int32, (PAIR, rows), 0) < HEAD_DIM
    grad_query = []
    for pr in range(pairs):
        cols = pl.ds(pr * PAIR, PAIR)
        acc = jnp.zeros((PAIR, rows), F32)
        for slot in order:
            prob = ew[slot, pr] * scale[slot, pr]
            grad_score = (prob * (dp[slot, pr] - dots[pr])).astype(BF16)
            key_t = kv[slot, 0, :, cols].astype(F32).T
            key_m = jnp.concatenate(
                [jnp.where(low_row, key_t, 0.0), jnp.where(low_row, 0.0, key_t)], axis=1
            ).astype(BF16)
            stacked = jnp.concatenate([grad_score[:, :rows], grad_score[:, rows:]], axis=0)
            acc = acc + dot_nn(key_m, stacked)
            if slot == REACH:
                dk[pr] = dot_nn(grad_score, qbd[slot, pr])
                dv[pr] = dot_nn(prob.astype(BF16), gbd[slot, pr])
        grad_query.append((acc * (HEAD_DIM**-0.5)).T.astype(BF16))
    query_all = jnp.concatenate(grad_query, axis=1)
    part[...] = dot_nt(query_all, wq[...])

    others = (0, 2 * REACH, 1, 3)
    for slot in others:
        wait_from(qg_out, slot)
        spread(slot)
        for pr in range(pairs):
            cols = pl.ds(pr * PAIR, PAIR)
            s2[slot, pr] = dot_nt(kv[REACH, 0, :, cols], qbd[slot, pr]) * LOG2E
            dp2[slot, pr] = dot_nt(kv[REACH, 1, :, cols], gbd[slot, pr])

    def query_tile(slot):
        for pr in range(pairs):
            shift = st_in[slot, pr, pl.ds(0, groups), :]
            row_dot = st_in[slot, pr, pl.ds(groups, 1), :]
            prob = jnp.exp2(grouped(s2[slot, pr]) + shift[:, None, :]).reshape(rows, 2 * rows)
            grad_score = (prob * (dp2[slot, pr] - row_dot)).astype(BF16)
            dk[pr] += dot_nn(grad_score, qbd[slot, pr])
            dv[pr] += dot_nn(prob.astype(BF16), gbd[slot, pr])

    wait_from(st_out, others[0])
    query_tile(others[0])
    wait_from(st_out, others[1])
    query_tile(others[1])
    wait_from(st_out, others[2])
    query_tile(others[2])
    wait_from(st_out, others[3])
    query_tile(others[3])
    key_all = jnp.concatenate([dk[pr].astype(BF16) for pr in range(pairs)], axis=1)
    value_all = jnp.concatenate([dv[pr].astype(BF16) for pr in range(pairs)], axis=1)

    def share(j):
        lines = pl.ds(pl.multiple_of(j * feats, feats), feats)
        return (
            part[:, lines]
            + dot_nt(key_all, wk[lines, :])
            + dot_nt(value_all, wv[lines, :])
        )

    red_out = []
    for i, peer in enumerate(peers):
        red_src[i] = share(peer).astype(BF16)
        copy = pltpu.make_async_remote_copy(
            src_ref=red_src.at[i],
            dst_ref=red_in.at[i],
            send_sem=red_send.at[i],
            recv_sem=red_recv.at[i],
            device_id=(me, peer),
            device_id_type=MESH,
        )
        copy.start()
        red_out.append(copy)
    total = share(head)
    for i in (2, 0, 1):
        red_out[i].wait_recv()
        total = total + red_in[i].astype(F32)
    out_ref[...] = total.astype(out_ref.dtype)
    for copy in (*kv_out, *qg_out, *st_out, *red_out):
        copy.wait_send()


def solution(mesh):
    nb = mesh.shape["blk"]

    def body(vertices, grad_out, w_query, w_key, w_value, w_out, pair_bins, bias_table, head_index):
        rows, width = vertices.shape
        feats = w_query.shape[1]
        pairs = feats // PAIR
        vmem, smem, dma = pltpu.VMEM, pltpu.SMEM, pltpu.SemaphoreType.DMA
        scratch = [
            vmem((rows, width), BF16),
            vmem((rows, width), BF16),
            vmem((width, feats), BF16),
            vmem((width, feats), BF16),
            vmem((width, feats), BF16),
            vmem((feats, width), BF16),
            smem(pair_bins.shape, jnp.int32),
            smem(bias_table.shape, F32),
            smem(head_index.shape, jnp.int32),
            vmem((WIDTH, 2, rows, feats), BF16),
            vmem((WIDTH, 2, rows, feats), BF16),
            vmem((WIDTH, pairs, 2 * rows, PAIR), BF16),
            vmem((WIDTH, pairs, 2 * rows, PAIR), BF16),
            vmem((WIDTH, pairs, rows, 2 * rows), F32),
            vmem((WIDTH, pairs, rows, 2 * rows), F32),
            vmem((WIDTH, pairs, rows, 2 * rows), F32),
            vmem((WIDTH, pairs, rows, 2 * rows), F32),
            vmem((WIDTH, pairs, rows // GROUP, 2 * rows), F32),
            vmem((WIDTH, pairs, 8, 2 * rows), F32),
            vmem((WIDTH, pairs, 8, 2 * rows), F32),
            vmem((pairs, rows, PAIR), F32),
            vmem((pairs, rows, PAIR), F32),
            vmem((rows, width), F32),
            vmem((3, rows, feats), BF16),
            vmem((3, rows, feats), BF16),
            dma((9,)),
            dma((4,)), dma((WIDTH,)),
            dma((4,)), dma((WIDTH,)),
            dma((4,)), dma((WIDTH,)),
            dma((3,)), dma((3,)),
        ]
        return pl.pallas_call(
            functools.partial(kernel, nb),
            out_shape=jax.ShapeDtypeStruct((rows, feats), BF16),
            in_specs=[pl.BlockSpec(memory_space=pltpu.MemorySpace.HBM)] * 9,
            out_specs=pl.BlockSpec(memory_space=pltpu.VMEM),
            scratch_shapes=scratch,
            compiler_params=pltpu.CompilerParams(
                collective_id=0, has_side_effects=True, vmem_limit_bytes=63 * 2**20 + 2**19
            ),
            name="attend_backward",
        )(vertices, grad_out, w_query, w_key, w_value, w_out, pair_bins, bias_table, head_index)

    in_specs = (
        P("blk", None),
        P("blk", None),
        P(None, "head"),
        P(None, "head"),
        P(None, "head"),
        P("head", None),
        P("blk", None),
        P(),
        P("head"),
    )
    return jax.shard_map(body, mesh=mesh, in_specs=in_specs, out_specs=P("blk", "head"), check_vma=False)
```

```python
import functools
import math

import jax
import jax.numpy as jnp
from jax import lax
from jax.experimental import pallas as pl
from jax.experimental.pallas import tpu as pltpu
from jax.sharding import PartitionSpec as P

HEAD_DIM = 64
REACH = 2
GROUP = 32
WIDTH = 2 * REACH + 1
PAIR = 2 * HEAD_DIM
LOG2E = math.log2(math.e)
MESH = pl.DeviceIdType.MESH
F32 = jnp.float32
BF16 = jnp.bfloat16
NEAR = (1, -1, 2, -2)


def dot_nn(a, b):
    return lax.dot_general(a, b, (((1,), (0,)), ((), ())), preferred_element_type=F32)


def dot_nt(a, b):
    return lax.dot_general(a, b, (((1,), (1,)), ((), ())), preferred_element_type=F32)


def kernel(
    nb,
    x_hbm, g_hbm, wq_hbm, wk_hbm, wv_hbm, wo_hbm, bins_hbm, table_hbm, hid_hbm,
    out_ref,
    x, g, wq, wk, wv, wo, bins, table, hid,
    kv, qg, qbd, gbd, ew, dp, s2, dp2, bias, bias_in, st_src, st_in, dk, dv, part, red_src, red_in,
    in_sem, kv_send, kv_recv, qg_send, qg_recv, bias_send, bias_recv, st_send, st_recv, red_send, red_recv,
):
    rows = x.shape[0]
    feats = wq.shape[1]
    pairs = feats // PAIR
    groups = rows // GROUP
    me = lax.axis_index("blk")
    head = lax.axis_index("head")
    peers = (lax.rem(head + 2, 4), 3 - head, head + 1 - 2 * lax.rem(head, 2))

    def block(by):
        return lax.rem(me + (by + nb), nb)

    barrier = pltpu.get_barrier_semaphore()
    for by in NEAR:
        pl.semaphore_signal(barrier, inc=1, device_id=(block(by), head), device_id_type=MESH)
    for peer in peers:
        pl.semaphore_signal(barrier, inc=1, device_id=(me, peer), device_id_type=MESH)

    loads = [
        pltpu.make_async_copy(src, dst, in_sem.at[i])
        for i, (src, dst) in enumerate(
            (
                (x_hbm, x), (wk_hbm, wk), (wv_hbm, wv), (wq_hbm, wq), (g_hbm, g), (wo_hbm, wo),
                (bins_hbm, bins), (table_hbm, table), (hid_hbm, hid),
            )
        )
    ]
    for load in loads[:3]:
        load.start()

    def to_block(src, dst, send, recv, i):
        by = NEAR[i]
        return pltpu.make_async_remote_copy(
            src_ref=src,
            dst_ref=dst.at[REACH - by],
            send_sem=send.at[i],
            recv_sem=recv.at[REACH - by],
            device_id=(block(by), head),
            device_id_type=MESH,
        )

    def wait_from(copies, slot):
        copies[NEAR.index(REACH - slot)].wait_recv()

    loads[0].wait()
    loads[1].wait()
    for load in loads[3:]:
        load.start()
    kv[REACH, 0] = dot_nn(x[...], wk[...]).astype(BF16)
    loads[2].wait()
    kv[REACH, 1] = dot_nn(x[...], wv[...]).astype(BF16)
    pl.semaphore_wait(barrier, len(NEAR) + len(peers))
    kv_out = [to_block(kv.at[REACH], kv, kv_send, kv_recv, i) for i in range(len(NEAR))]
    for copy in kv_out:
        copy.start()
    loads[3].wait()
    qg[REACH, 0] = (dot_nn(x[...], wq[...]).astype(BF16).astype(F32) * (HEAD_DIM**-0.5)).astype(BF16)
    loads[4].wait()
    loads[5].wait()
    qg[REACH, 1] = dot_nt(g[...], wo[...]).astype(BF16)
    low_lane = lax.broadcasted_iota(jnp.int32, (rows, PAIR), 1) < HEAD_DIM
    zero = jnp.zeros((rows, PAIR), BF16)

    def spread(slot):
        for pr in range(pairs):
            cols = pl.ds(pr * PAIR, PAIR)
            for which, dst in ((0, qbd), (1, gbd)):
                both = qg[slot, which, :, cols]
                dst[slot, pr, pl.ds(0, rows), :] = jnp.where(low_lane, both, zero)
                dst[slot, pr, pl.ds(rows, rows), :] = jnp.where(low_lane, zero, both)

    spread(REACH)

    loads[6].wait()
    loads[7].wait()
    loads[8].wait()
    lane_group = lax.broadcasted_iota(jnp.int32, (1, rows), 1) // GROUP

    def bias_rows(slot, carry):
        for h in range(2 * pairs):
            lines = []
            for kg in range(groups):
                line = jnp.zeros((1, rows), F32)
                for gr in range(groups):
                    line = jnp.where(lane_group == gr, table[hid[h], bins[gr, slot * groups + kg]], line)
                lines.append(line)
            bias[slot, h // 2, :, pl.ds((h % 2) * rows, rows)] = jnp.concatenate(lines, axis=0) * LOG2E
        return carry

    lax.fori_loop(0, WIDTH, bias_rows, 0)

    def grouped(tile):
        return tile.reshape(groups, GROUP, 2 * rows)

    stats = {}

    def key_tile(slot):
        for pr in range(pairs):
            cols = pl.ds(pr * PAIR, PAIR)
            score = dot_nt(kv[slot, 0, :, cols], qbd[REACH, pr])
            weigh = dot_nt(kv[slot, 1, :, cols], gbd[REACH, pr])
            shift = bias[slot, pr]
            logit = grouped(score) * LOG2E + shift[:, None, :]
            peak = jnp.max(logit, axis=(0, 1), keepdims=True)
            expo = jnp.exp2(logit - peak).reshape(rows, 2 * rows)
            ew[slot, pr] = expo
            dp[slot, pr] = weigh
            total = jnp.sum(expo, axis=0, keepdims=True)
            cross = jnp.sum(expo * weigh, axis=0, keepdims=True)
            stats[slot, pr] = (peak.reshape(1, 2 * rows), total, cross)

    order = (REACH, 0, 2 * REACH, 1, 3)
    key_tile(REACH)
    qg_out = [to_block(qg.at[REACH], qg, qg_send, qg_recv, i) for i in range(len(NEAR))]
    bias_out = [to_block(bias.at[REACH + NEAR[i]], bias_in, bias_send, bias_recv, i) for i in range(len(NEAR))]
    for copy in kv_out:
        copy.wait_send()
    for copy in (*qg_out, *bias_out):
        copy.start()
    wait_from(kv_out, order[1])
    key_tile(order[1])
    wait_from(kv_out, order[2])
    key_tile(order[2])
    wait_from(kv_out, order[3])
    key_tile(order[3])
    wait_from(kv_out, order[4])
    key_tile(order[4])

    scale = {}
    dots = []
    for pr in range(pairs):
        top = functools.reduce(jnp.maximum, [stats[s, pr][0] for s in range(WIDTH)])
        lift = [jnp.exp2(stats[s, pr][0] - top) for s in range(WIDTH)]
        total = sum(stats[s, pr][1] * lift[s] for s in range(WIDTH))
        cross = sum(stats[s, pr][2] * lift[s] for s in range(WIDTH))
        inverse = 1.0 / total
        lse = top + jnp.log2(total)
        row_dot = cross * inverse
        dots.append(row_dot)
        for s in range(WIDTH):
            scale[s, pr] = lift[s] * inverse
        for half in range(2):
            cols = slice(half * rows, (half + 1) * rows)
            st_src[pl.ds(2 * pr + half, 1), :] = lse[:, cols]
            st_src[pl.ds(2 * (pairs + pr) + half, 1), :] = row_dot[:, cols]
    st_out = [to_block(st_src, st_in, st_send, st_recv, i) for i in range(len(NEAR))]
    for copy in st_out:
        copy.start()

    low_row = lax.broadcasted_iota(jnp.int32, (PAIR, rows), 0) < HEAD_DIM
    grad_query = []
    for pr in range(pairs):
        cols = pl.ds(pr * PAIR, PAIR)
        acc = jnp.zeros((PAIR, rows), F32)
        for slot in order:
            prob = ew[slot, pr] * scale[slot, pr]
            grad_score = (prob * (dp[slot, pr] - dots[pr])).astype(BF16)
            key_t = kv[slot, 0, :, cols].astype(F32).T
            key_m = jnp.concatenate(
                [jnp.where(low_row, key_t, 0.0), jnp.where(low_row, 0.0, key_t)], axis=1
            ).astype(BF16)
            stacked = jnp.concatenate([grad_score[:, :rows], grad_score[:, rows:]], axis=0)
            acc = acc + dot_nn(key_m, stacked)
            if slot == REACH:
                dk[pr] = dot_nn(grad_score, qbd[slot, pr])
                dv[pr] = dot_nn(prob.astype(BF16), gbd[slot, pr])
        grad_query.append((acc * (HEAD_DIM**-0.5)).T.astype(BF16))
    query_all = jnp.concatenate(grad_query, axis=1)
    part[...] = dot_nt(query_all, wq[...])

    others = (0, 2 * REACH, 1, 3)
    for slot in others:
        wait_from(qg_out, slot)
        wait_from(bias_out, slot)
        spread(slot)
        for pr in range(pairs):
            cols = pl.ds(pr * PAIR, PAIR)
            score = dot_nt(kv[REACH, 0, :, cols], qbd[slot, pr])
            s2[slot, pr] = (grouped(score) * LOG2E + bias_in[slot, pr][:, None, :]).reshape(rows, 2 * rows)
            dp2[slot, pr] = dot_nt(kv[REACH, 1, :, cols], gbd[slot, pr])

    def query_tile(slot):
        for pr in range(pairs):
            lse, row_dot = (
                jnp.concatenate([st_in[slot, pl.ds(2 * at + half, 1), :] for half in range(2)], axis=1)
                for at in (pr, pairs + pr)
            )
            prob = jnp.exp2(s2[slot, pr] - lse)
            grad_score = (prob * (dp2[slot, pr] - row_dot)).astype(BF16)
            dk[pr] += dot_nn(grad_score, qbd[slot, pr])
            dv[pr] += dot_nn(prob.astype(BF16), gbd[slot, pr])

    wait_from(st_out, others[0])
    query_tile(others[0])
    wait_from(st_out, others[1])
    query_tile(others[1])
    wait_from(st_out, others[2])
    query_tile(others[2])
    wait_from(st_out, others[3])
    query_tile(others[3])
    key_all = jnp.concatenate([dk[pr].astype(BF16) for pr in range(pairs)], axis=1)
    value_all = jnp.concatenate([dv[pr].astype(BF16) for pr in range(pairs)], axis=1)

    def share(j):
        lines = pl.ds(pl.multiple_of(j * feats, feats), feats)
        return (
            part[:, lines]
            + dot_nt(key_all, wk[lines, :])
            + dot_nt(value_all, wv[lines, :])
        )

    red_out = []
    for i, peer in enumerate(peers):
        red_src[i] = share(peer).astype(BF16)
        copy = pltpu.make_async_remote_copy(
            src_ref=red_src.at[i],
            dst_ref=red_in.at[i],
            send_sem=red_send.at[i],
            recv_sem=red_recv.at[i],
            device_id=(me, peer),
            device_id_type=MESH,
        )
        copy.start()
        red_out.append(copy)
    total = share(head)
    for i in (2, 0, 1):
        red_out[i].wait_recv()
        total = total + red_in[i].astype(F32)
    out_ref[...] = total.astype(out_ref.dtype)
    for copy in (*qg_out, *bias_out, *st_out, *red_out):
        copy.wait_send()


def solution(mesh):
    nb = mesh.shape["blk"]

    def body(vertices, grad_out, w_query, w_key, w_value, w_out, pair_bins, bias_table, head_index):
        rows, width = vertices.shape
        feats = w_query.shape[1]
        pairs = feats // PAIR
        vmem, smem, dma = pltpu.VMEM, pltpu.SMEM, pltpu.SemaphoreType.DMA
        scratch = [
            vmem((rows, width), BF16),
            vmem((rows, width), BF16),
            vmem((width, feats), BF16),
            vmem((width, feats), BF16),
            vmem((width, feats), BF16),
            vmem((feats, width), BF16),
            smem(pair_bins.shape, jnp.int32),
            smem(bias_table.shape, F32),
            smem(head_index.shape, jnp.int32),
            vmem((WIDTH, 2, rows, feats), BF16),
            vmem((WIDTH, 2, rows, feats), BF16),
            vmem((WIDTH, pairs, 2 * rows, PAIR), BF16),
            vmem((WIDTH, pairs, 2 * rows, PAIR), BF16),
            vmem((WIDTH, pairs, rows, 2 * rows), F32),
            vmem((WIDTH, pairs, rows, 2 * rows), F32),
            vmem((WIDTH, pairs, rows, 2 * rows), F32),
            vmem((WIDTH, pairs, rows, 2 * rows), F32),
            vmem((WIDTH, pairs, rows // GROUP, 2 * rows), F32),
            vmem((WIDTH, pairs, rows // GROUP, 2 * rows), F32),
            vmem((4 * pairs, rows), F32),
            vmem((WIDTH, 4 * pairs, rows), F32),
            vmem((pairs, rows, PAIR), F32),
            vmem((pairs, rows, PAIR), F32),
            vmem((rows, width), F32),
            vmem((3, rows, feats), BF16),
            vmem((3, rows, feats), BF16),
            dma((9,)),
            dma((4,)), dma((WIDTH,)),
            dma((4,)), dma((WIDTH,)),
            dma((4,)), dma((WIDTH,)),
            dma((4,)), dma((WIDTH,)),
            dma((3,)), dma((3,)),
        ]
        return pl.pallas_call(
            functools.partial(kernel, nb),
            out_shape=pltpu.VMEM((rows, feats), BF16),
            in_specs=[pl.BlockSpec(memory_space=pl.ANY)] * 9,
            out_specs=pl.BlockSpec(memory_space=pltpu.VMEM),
            scratch_shapes=scratch,
            compiler_params=pltpu.CompilerParams(
                collective_id=0, has_side_effects=True, vmem_limit_bytes=32 * 2**20
            ),
            name="attend_backward",
        )(*(pltpu.with_memory_space_constraint(a, pltpu.HBM) for a in (
            vertices, grad_out, w_query, w_key, w_value, w_out, pair_bins, bias_table, head_index
        )))

    in_specs = (
        P("blk", None),
        P("blk", None),
        P(None, "head"),
        P(None, "head"),
        P(None, "head"),
        P("head", None),
        P("blk", None),
        P(),
        P("head"),
    )
    return jax.shard_map(body, mesh=mesh, in_specs=in_specs, out_specs=P("blk", "head"), check_vma=False)
```

```python
import functools
import math

import jax
import jax.numpy as jnp
from jax import lax
from jax.experimental import pallas as pl
from jax.experimental.pallas import tpu as pltpu
from jax.sharding import PartitionSpec as P

HEAD_DIM = 64
REACH = 2
GROUP = 32
WIDTH = 2 * REACH + 1
PAIR = 2 * HEAD_DIM
LOG2E = math.log2(math.e)
MESH = pl.DeviceIdType.MESH
F32 = jnp.float32
BF16 = jnp.bfloat16


def dot_nn(a, b):
    return lax.dot_general(a, b, (((1,), (0,)), ((), ())), preferred_element_type=F32)


def dot_nt(a, b):
    return lax.dot_general(a, b, (((1,), (1,)), ((), ())), preferred_element_type=F32)


def kernel(
    nb,
    x_hbm, g_hbm, wq_hbm, wk_hbm, wv_hbm, wo_hbm, bins_hbm, table_hbm, hid_hbm,
    out_ref,
    x, g, wq, wk, wv, wo, bins, table, hid,
    kv, qg, qbd, gbd, ew, dp, s2, dp2, bias, bias_in, st_src, st_in, dk, dv, part, red_src, red_in,
    in_sem, kv_send, kv_recv, qg_send, qg_recv, bias_send, bias_recv, st_send, st_recv, red_send, red_recv,
):
    rows = x.shape[0]
    feats = wq.shape[1]
    pairs = feats // PAIR
    groups = rows // GROUP
    me = lax.axis_index("blk")
    head = lax.axis_index("head")
    peers = (lax.rem(head + 2, 4), 3 - head, head + 1 - 2 * lax.rem(head, 2))

    def block(by):
        return lax.rem(me + (by + nb), nb)

    far = 2 * lax.rem(me, 2) - 1
    near = (far, -far, REACH, -REACH)
    barrier = pltpu.get_barrier_semaphore()
    for by in near:
        pl.semaphore_signal(barrier, inc=1, device_id=(block(by), head), device_id_type=MESH)
    for peer in peers:
        pl.semaphore_signal(barrier, inc=1, device_id=(me, peer), device_id_type=MESH)

    loads = [
        pltpu.make_async_copy(src, dst, in_sem.at[i])
        for i, (src, dst) in enumerate(
            (
                (x_hbm, x), (wk_hbm, wk), (wv_hbm, wv), (wq_hbm, wq), (g_hbm, g), (wo_hbm, wo),
                (bins_hbm, bins), (table_hbm, table), (hid_hbm, hid),
            )
        )
    ]
    for load in loads[:3]:
        load.start()

    def to_block(src, dst, send, recv, i):
        by = near[i]
        return pltpu.make_async_remote_copy(
            src_ref=src,
            dst_ref=dst.at[REACH - by],
            send_sem=send.at[i],
            recv_sem=recv.at[REACH - by],
            device_id=(block(by), head),
            device_id_type=MESH,
        )

    slots = (REACH, *(REACH - by for by in near))

    def wait_from(copies, tile):
        copies[tile - 1].wait_recv()

    loads[0].wait()
    loads[1].wait()
    for load in loads[3:]:
        load.start()
    kv[REACH, 0] = dot_nn(x[...], wk[...]).astype(BF16)
    loads[2].wait()
    kv[REACH, 1] = dot_nn(x[...], wv[...]).astype(BF16)
    pl.semaphore_wait(barrier, len(near) + len(peers))
    kv_out = [to_block(kv.at[REACH], kv, kv_send, kv_recv, i) for i in range(len(near))]
    for copy in kv_out:
        copy.start()
    loads[3].wait()
    qg[REACH, 0] = (dot_nn(x[...], wq[...]).astype(BF16).astype(F32) * (HEAD_DIM**-0.5)).astype(BF16)
    loads[4].wait()
    loads[5].wait()
    qg[REACH, 1] = dot_nt(g[...], wo[...]).astype(BF16)
    low_lane = lax.broadcasted_iota(jnp.int32, (rows, PAIR), 1) < HEAD_DIM
    zero = jnp.zeros((rows, PAIR), BF16)

    def spread(tile):
        for pr in range(pairs):
            cols = pl.ds(pr * PAIR, PAIR)
            for which, dst in ((0, qbd), (1, gbd)):
                both = qg[slots[tile], which, :, cols]
                dst[tile, pr, pl.ds(0, rows), :] = jnp.where(low_lane, both, zero)
                dst[tile, pr, pl.ds(rows, rows), :] = jnp.where(low_lane, zero, both)

    spread(0)

    loads[6].wait()
    loads[7].wait()
    loads[8].wait()
    lane_group = lax.broadcasted_iota(jnp.int32, (1, rows), 1) // GROUP

    def bias_rows(slot, carry):
        for h in range(2 * pairs):
            lines = []
            for kg in range(groups):
                line = jnp.zeros((1, rows), F32)
                for gr in range(groups):
                    line = jnp.where(lane_group == gr, table[hid[h], bins[gr, slot * groups + kg]], line)
                lines.append(line)
            bias[slot, h // 2, :, pl.ds((h % 2) * rows, rows)] = jnp.concatenate(lines, axis=0) * LOG2E
        return carry

    lax.fori_loop(0, WIDTH, bias_rows, 0)

    def grouped(tile):
        return tile.reshape(groups, GROUP, 2 * rows)

    stats = {}

    def key_tile(tile):
        slot = slots[tile]
        for pr in range(pairs):
            cols = pl.ds(pr * PAIR, PAIR)
            score = dot_nt(kv[slot, 0, :, cols], qbd[0, pr])
            weigh = dot_nt(kv[slot, 1, :, cols], gbd[0, pr])
            shift = bias[slot, pr]
            logit = grouped(score) * LOG2E + shift[:, None, :]
            peak = jnp.max(logit, axis=(0, 1), keepdims=True)
            expo = jnp.exp2(logit - peak).reshape(rows, 2 * rows)
            ew[tile, pr] = expo
            dp[tile, pr] = weigh
            total = jnp.sum(expo, axis=0, keepdims=True)
            cross = jnp.sum(expo * weigh, axis=0, keepdims=True)
            stats[tile, pr] = (peak.reshape(1, 2 * rows), total, cross)

    order = (0, 3, 4, 1, 2)
    key_tile(0)
    qg_out = [to_block(qg.at[REACH], qg, qg_send, qg_recv, i) for i in range(len(near))]
    bias_out = [to_block(bias.at[REACH + near[i]], bias_in, bias_send, bias_recv, i) for i in range(len(near))]
    for copy in kv_out:
        copy.wait_send()
    for copy in (*qg_out, *bias_out):
        copy.start()
    wait_from(kv_out, order[1])
    key_tile(order[1])
    wait_from(kv_out, order[2])
    key_tile(order[2])
    wait_from(kv_out, order[3])
    key_tile(order[3])
    wait_from(kv_out, order[4])
    key_tile(order[4])

    scale = {}
    dots = []
    for pr in range(pairs):
        top = functools.reduce(jnp.maximum, [stats[s, pr][0] for s in range(WIDTH)])
        lift = [jnp.exp2(stats[s, pr][0] - top) for s in range(WIDTH)]
        total = sum(stats[s, pr][1] * lift[s] for s in range(WIDTH))
        cross = sum(stats[s, pr][2] * lift[s] for s in range(WIDTH))
        inverse = 1.0 / total
        lse = top + jnp.log2(total)
        row_dot = cross * inverse
        dots.append(row_dot)
        for s in range(WIDTH):
            scale[s, pr] = lift[s] * inverse
        for half in range(2):
            cols = slice(half * rows, (half + 1) * rows)
            st_src[pl.ds(2 * pr + half, 1), :] = lse[:, cols]
            st_src[pl.ds(2 * (pairs + pr) + half, 1), :] = row_dot[:, cols]
    st_out = [to_block(st_src, st_in, st_send, st_recv, i) for i in range(len(near))]
    for copy in st_out:
        copy.start()

    low_row = lax.broadcasted_iota(jnp.int32, (PAIR, rows), 0) < HEAD_DIM
    grad_query = []
    for pr in range(pairs):
        cols = pl.ds(pr * PAIR, PAIR)
        acc = jnp.zeros((PAIR, rows), F32)
        for tile in order:
            prob = ew[tile, pr] * scale[tile, pr]
            grad_score = (prob * (dp[tile, pr] - dots[pr])).astype(BF16)
            key_t = kv[slots[tile], 0, :, cols].astype(F32).T
            key_m = jnp.concatenate(
                [jnp.where(low_row, key_t, 0.0), jnp.where(low_row, 0.0, key_t)], axis=1
            ).astype(BF16)
            stacked = jnp.concatenate([grad_score[:, :rows], grad_score[:, rows:]], axis=0)
            acc = acc + dot_nn(key_m, stacked)
            if tile == 0:
                dk[pr] = dot_nn(grad_score, qbd[0, pr])
                dv[pr] = dot_nn(prob.astype(BF16), gbd[0, pr])
        grad_query.append((acc * (HEAD_DIM**-0.5)).T.astype(BF16))
    query_all = jnp.concatenate(grad_query, axis=1)
    part[...] = dot_nt(query_all, wq[...])

    others = (3, 4, 1, 2)
    for tile in others:
        slot = slots[tile]
        wait_from(qg_out, tile)
        wait_from(bias_out, tile)
        spread(tile)
        for pr in range(pairs):
            cols = pl.ds(pr * PAIR, PAIR)
            score = dot_nt(kv[REACH, 0, :, cols], qbd[tile, pr])
            s2[tile, pr] = (grouped(score) * LOG2E + bias_in[slot, pr][:, None, :]).reshape(rows, 2 * rows)
            dp2[tile, pr] = dot_nt(kv[REACH, 1, :, cols], gbd[tile, pr])

    def query_tile(tile):
        slot = slots[tile]
        for pr in range(pairs):
            lse, row_dot = (
                jnp.concatenate([st_in[slot, pl.ds(2 * at + half, 1), :] for half in range(2)], axis=1)
                for at in (pr, pairs + pr)
            )
            prob = jnp.exp2(s2[tile, pr] - lse)
            grad_score = (prob * (dp2[tile, pr] - row_dot)).astype(BF16)
            dk[pr] += dot_nn(grad_score, qbd[tile, pr])
            dv[pr] += dot_nn(prob.astype(BF16), gbd[tile, pr])

    wait_from(st_out, others[0])
    query_tile(others[0])
    wait_from(st_out, others[1])
    query_tile(others[1])
    wait_from(st_out, others[2])
    query_tile(others[2])
    wait_from(st_out, others[3])
    query_tile(others[3])
    key_all = jnp.concatenate([dk[pr].astype(BF16) for pr in range(pairs)], axis=1)
    value_all = jnp.concatenate([dv[pr].astype(BF16) for pr in range(pairs)], axis=1)

    def share(j):
        lines = pl.ds(pl.multiple_of(j * feats, feats), feats)
        return (
            part[:, lines]
            + dot_nt(key_all, wk[lines, :])
            + dot_nt(value_all, wv[lines, :])
        )

    red_out = []
    for i, peer in enumerate(peers):
        red_src[i] = share(peer).astype(BF16)
        copy = pltpu.make_async_remote_copy(
            src_ref=red_src.at[i],
            dst_ref=red_in.at[i],
            send_sem=red_send.at[i],
            recv_sem=red_recv.at[i],
            device_id=(me, peer),
            device_id_type=MESH,
        )
        copy.start()
        red_out.append(copy)
    total = share(head)
    for i in (2, 0, 1):
        red_out[i].wait_recv()
        total = total + red_in[i].astype(F32)
    out_ref[...] = total.astype(out_ref.dtype)
    for copy in (*qg_out, *bias_out, *st_out, *red_out):
        copy.wait_send()


def solution(mesh):
    nb = mesh.shape["blk"]

    def body(vertices, grad_out, w_query, w_key, w_value, w_out, pair_bins, bias_table, head_index):
        rows, width = vertices.shape
        feats = w_query.shape[1]
        pairs = feats // PAIR
        vmem, smem, dma = pltpu.VMEM, pltpu.SMEM, pltpu.SemaphoreType.DMA
        scratch = [
            vmem((rows, width), BF16),
            vmem((rows, width), BF16),
            vmem((width, feats), BF16),
            vmem((width, feats), BF16),
            vmem((width, feats), BF16),
            vmem((feats, width), BF16),
            smem(pair_bins.shape, jnp.int32),
            smem(bias_table.shape, F32),
            smem(head_index.shape, jnp.int32),
            vmem((WIDTH, 2, rows, feats), BF16),
            vmem((WIDTH, 2, rows, feats), BF16),
            vmem((WIDTH, pairs, 2 * rows, PAIR), BF16),
            vmem((WIDTH, pairs, 2 * rows, PAIR), BF16),
            vmem((WIDTH, pairs, rows, 2 * rows), F32),
            vmem((WIDTH, pairs, rows, 2 * rows), F32),
            vmem((WIDTH, pairs, rows, 2 * rows), F32),
            vmem((WIDTH, pairs, rows, 2 * rows), F32),
            vmem((WIDTH, pairs, rows // GROUP, 2 * rows), F32),
            vmem((WIDTH, pairs, rows // GROUP, 2 * rows), F32),
            vmem((4 * pairs, rows), F32),
            vmem((WIDTH, 4 * pairs, rows), F32),
            vmem((pairs, rows, PAIR), F32),
            vmem((pairs, rows, PAIR), F32),
            vmem((rows, width), F32),
            vmem((3, rows, feats), BF16),
            vmem((3, rows, feats), BF16),
            dma((9,)),
            dma((4,)), dma((WIDTH,)),
            dma((4,)), dma((WIDTH,)),
            dma((4,)), dma((WIDTH,)),
            dma((4,)), dma((WIDTH,)),
            dma((3,)), dma((3,)),
        ]
        return pl.pallas_call(
            functools.partial(kernel, nb),
            out_shape=pltpu.VMEM((rows, feats), BF16),
            in_specs=[pl.BlockSpec(memory_space=pl.ANY)] * 9,
            out_specs=pl.BlockSpec(memory_space=pltpu.VMEM),
            scratch_shapes=scratch,
            compiler_params=pltpu.CompilerParams(
                collective_id=0, has_side_effects=True, vmem_limit_bytes=32 * 2**20
            ),
            name="attend_backward",
        )(*(pltpu.with_memory_space_constraint(a, pltpu.HBM) for a in (
            vertices, grad_out, w_query, w_key, w_value, w_out, pair_bins, bias_table, head_index
        )))

    in_specs = (
        P("blk", None),
        P("blk", None),
        P(None, "head"),
        P(None, "head"),
        P(None, "head"),
        P("head", None),
        P("blk", None),
        P(),
        P("head"),
    )
    return jax.shard_map(body, mesh=mesh, in_specs=in_specs, out_specs=P("blk", "head"), check_vma=False)
```

```python
import functools
import math

import jax
import jax.numpy as jnp
from jax import lax
from jax.experimental import pallas as pl
from jax.experimental.pallas import tpu as pltpu
from jax.sharding import PartitionSpec as P

HEAD_DIM = 64
REACH = 2
GROUP = 32
WIDTH = 2 * REACH + 1
PAIR = 2 * HEAD_DIM
LOG2E = math.log2(math.e)
MESH = pl.DeviceIdType.MESH
F32 = jnp.float32
BF16 = jnp.bfloat16


def dot_nn(a, b):
    return lax.dot_general(a, b, (((1,), (0,)), ((), ())), preferred_element_type=F32)


def dot_nt(a, b):
    return lax.dot_general(a, b, (((1,), (1,)), ((), ())), preferred_element_type=F32)


def kernel(
    nb,
    x_hbm, g_hbm, wq_hbm, wk_hbm, wv_hbm, wo_hbm, bins_hbm, table_hbm, hid_hbm,
    out_ref,
    x, g, wq, wk, wv, wo, bins, table, hid,
    kv, qg, qbd, gbd, ew, dp, s2, dp2, bias, bias_in, st_src, st_in, dk, dv, part, red_src, red_in, turned,
    in_sem, kv_send, kv_recv, qg_send, qg_recv, bias_send, bias_recv, st_send, st_recv, red_send, red_recv,
):
    rows = x.shape[0]
    feats = wq.shape[1]
    pairs = feats // PAIR
    groups = rows // GROUP
    me = lax.axis_index("blk")
    head = lax.axis_index("head")
    peers = (lax.rem(head + 2, 4), 3 - head, head + 1 - 2 * lax.rem(head, 2))

    def block(by):
        return lax.rem(me + (by + nb), nb)

    far = 2 * lax.rem(me, 2) - 1
    near = (far, -far, REACH, -REACH)
    barrier = pltpu.get_barrier_semaphore()
    for by in near:
        pl.semaphore_signal(barrier, inc=1, device_id=(block(by), head), device_id_type=MESH)
    for peer in peers:
        pl.semaphore_signal(barrier, inc=1, device_id=(me, peer), device_id_type=MESH)

    loads = [
        pltpu.make_async_copy(src, dst, in_sem.at[i])
        for i, (src, dst) in enumerate(
            (
                (x_hbm, x), (wk_hbm, wk), (wv_hbm, wv), (wq_hbm, wq), (g_hbm, g), (wo_hbm, wo),
                (bins_hbm, bins), (table_hbm, table), (hid_hbm, hid),
            )
        )
    ]
    for load in loads[:3]:
        load.start()

    def to_block(src, dst, send, recv, i):
        by = near[i]
        return pltpu.make_async_remote_copy(
            src_ref=src,
            dst_ref=dst.at[REACH - by],
            send_sem=send.at[i],
            recv_sem=recv.at[REACH - by],
            device_id=(block(by), head),
            device_id_type=MESH,
        )

    slots = (REACH, *(REACH - by for by in near))

    def wait_from(copies, tile):
        copies[tile - 1].wait_recv()

    loads[0].wait()
    loads[1].wait()
    for load in loads[3:]:
        load.start()
    kv[REACH, 0] = dot_nn(x[...], wk[...]).astype(BF16)
    loads[2].wait()
    kv[REACH, 1] = dot_nn(x[...], wv[...]).astype(BF16)
    pl.semaphore_wait(barrier, len(near) + len(peers))
    kv_out = [to_block(kv.at[REACH], kv, kv_send, kv_recv, i) for i in range(len(near))]
    for copy in kv_out:
        copy.start()
    loads[3].wait()
    qg[REACH, 0] = (dot_nn(x[...], wq[...]).astype(BF16).astype(F32) * (HEAD_DIM**-0.5)).astype(BF16)
    loads[4].wait()
    loads[5].wait()
    qg[REACH, 1] = dot_nt(g[...], wo[...]).astype(BF16)
    low_lane = lax.broadcasted_iota(jnp.int32, (rows, PAIR), 1) < HEAD_DIM
    zero = jnp.zeros((rows, PAIR), BF16)

    def spread(tile):
        for pr in range(pairs):
            cols = pl.ds(pr * PAIR, PAIR)
            for which, dst in ((0, qbd), (1, gbd)):
                both = qg[slots[tile], which, :, cols]
                dst[tile, pr, pl.ds(0, rows), :] = jnp.where(low_lane, both, zero)
                dst[tile, pr, pl.ds(rows, rows), :] = jnp.where(low_lane, zero, both)

    spread(0)

    loads[6].wait()
    loads[7].wait()
    loads[8].wait()
    lane_group = lax.broadcasted_iota(jnp.int32, (1, rows), 1) // GROUP

    def bias_rows(slot, carry):
        for h in range(2 * pairs):
            lines = []
            for kg in range(groups):
                line = jnp.zeros((1, rows), F32)
                for gr in range(groups):
                    line = jnp.where(lane_group == gr, table[hid[h], bins[gr, slot * groups + kg]], line)
                lines.append(line)
            bias[slot, h // 2, :, pl.ds((h % 2) * rows, rows)] = jnp.concatenate(lines, axis=0) * LOG2E
        return carry

    lax.fori_loop(0, WIDTH, bias_rows, 0)

    def grouped(tile):
        return tile.reshape(groups, GROUP, 2 * rows)

    stats = {}

    def key_tile(tile):
        slot = slots[tile]
        for pr in range(pairs):
            cols = pl.ds(pr * PAIR, PAIR)
            score = dot_nt(kv[slot, 0, :, cols], qbd[0, pr])
            weigh = dot_nt(kv[slot, 1, :, cols], gbd[0, pr])
            shift = bias[slot, pr]
            logit = grouped(score) * LOG2E + shift[:, None, :]
            peak = jnp.max(logit, axis=(0, 1), keepdims=True)
            expo = jnp.exp2(logit - peak).reshape(rows, 2 * rows)
            ew[tile, pr] = expo
            dp[tile, pr] = weigh
            total = jnp.sum(expo, axis=0, keepdims=True)
            cross = jnp.sum(expo * weigh, axis=0, keepdims=True)
            stats[tile, pr] = (peak.reshape(1, 2 * rows), total, cross)

    order = (0, 3, 4, 1, 2)
    key_tile(0)
    qg_out = [to_block(qg.at[REACH], qg, qg_send, qg_recv, i) for i in range(len(near))]
    bias_out = [to_block(bias.at[REACH + near[i]], bias_in, bias_send, bias_recv, i) for i in range(len(near))]
    for copy in kv_out:
        copy.wait_send()
    for copy in (*qg_out, *bias_out):
        copy.start()
    wait_from(kv_out, order[1])
    key_tile(order[1])
    wait_from(kv_out, order[2])
    key_tile(order[2])
    for j in range(x.shape[1] // feats):
        lines = pl.ds(j * feats, feats)
        turned[j, pl.ds(0, feats), :] = wk[lines, :].T
        turned[j, pl.ds(feats, feats), :] = wv[lines, :].T
    wait_from(kv_out, order[3])
    key_tile(order[3])
    wait_from(kv_out, order[4])
    key_tile(order[4])

    scale = {}
    dots = []
    for pr in range(pairs):
        top = functools.reduce(jnp.maximum, [stats[s, pr][0] for s in range(WIDTH)])
        lift = [jnp.exp2(stats[s, pr][0] - top) for s in range(WIDTH)]
        total = sum(stats[s, pr][1] * lift[s] for s in range(WIDTH))
        cross = sum(stats[s, pr][2] * lift[s] for s in range(WIDTH))
        inverse = 1.0 / total
        lse = top + jnp.log2(total)
        row_dot = cross * inverse
        dots.append(row_dot)
        for s in range(WIDTH):
            scale[s, pr] = lift[s] * inverse
        for half in range(2):
            cols = slice(half * rows, (half + 1) * rows)
            st_src[pl.ds(2 * pr + half, 1), :] = lse[:, cols]
            st_src[pl.ds(2 * (pairs + pr) + half, 1), :] = row_dot[:, cols]
    st_out = [to_block(st_src, st_in, st_send, st_recv, i) for i in range(len(near))]
    for copy in st_out:
        copy.start()

    low_row = lax.broadcasted_iota(jnp.int32, (PAIR, rows), 0) < HEAD_DIM
    grad_query = []
    for pr in range(pairs):
        cols = pl.ds(pr * PAIR, PAIR)
        acc = jnp.zeros((PAIR, rows), F32)
        for tile in order:
            prob = ew[tile, pr] * scale[tile, pr]
            grad_score = (prob * (dp[tile, pr] - dots[pr])).astype(BF16)
            key_t = kv[slots[tile], 0, :, cols].astype(F32).T
            key_m = jnp.concatenate(
                [jnp.where(low_row, key_t, 0.0), jnp.where(low_row, 0.0, key_t)], axis=1
            ).astype(BF16)
            stacked = jnp.concatenate([grad_score[:, :rows], grad_score[:, rows:]], axis=0)
            acc = acc + dot_nn(key_m, stacked)
            if tile == 0:
                dk[pr] = dot_nn(grad_score, qbd[0, pr])
                dv[pr] = dot_nn(prob.astype(BF16), gbd[0, pr])
        grad_query.append((acc * (HEAD_DIM**-0.5)).T.astype(BF16))
    query_all = jnp.concatenate(grad_query, axis=1)
    part[...] = dot_nt(query_all, wq[...])

    others = (3, 4, 1, 2)
    for tile in others:
        slot = slots[tile]
        wait_from(qg_out, tile)
        wait_from(bias_out, tile)
        spread(tile)
        for pr in range(pairs):
            cols = pl.ds(pr * PAIR, PAIR)
            score = dot_nt(kv[REACH, 0, :, cols], qbd[tile, pr])
            s2[tile, pr] = (grouped(score) * LOG2E + bias_in[slot, pr][:, None, :]).reshape(rows, 2 * rows)
            dp2[tile, pr] = dot_nt(kv[REACH, 1, :, cols], gbd[tile, pr])

    def query_tile(tile):
        slot = slots[tile]
        for pr in range(pairs):
            lse, row_dot = (
                jnp.concatenate([st_in[slot, pl.ds(2 * at + half, 1), :] for half in range(2)], axis=1)
                for at in (pr, pairs + pr)
            )
            prob = jnp.exp2(s2[tile, pr] - lse)
            grad_score = (prob * (dp2[tile, pr] - row_dot)).astype(BF16)
            dk[pr] += dot_nn(grad_score, qbd[tile, pr])
            dv[pr] += dot_nn(prob.astype(BF16), gbd[tile, pr])

    wait_from(st_out, others[0])
    query_tile(others[0])
    wait_from(st_out, others[1])
    query_tile(others[1])
    wait_from(st_out, others[2])
    query_tile(others[2])
    wait_from(st_out, others[3])
    query_tile(others[3])
    key_all = jnp.concatenate([dk[pr].astype(BF16) for pr in range(pairs)], axis=1)
    value_all = jnp.concatenate([dv[pr].astype(BF16) for pr in range(pairs)], axis=1)

    both_all = jnp.concatenate([key_all, value_all], axis=1)

    def share(j):
        lines = pl.ds(pl.multiple_of(j * feats, feats), feats)
        return part[:, lines] + dot_nn(both_all, turned[j])

    red_out = []
    for i, peer in enumerate(peers):
        red_src[i] = share(peer).astype(BF16)
        copy = pltpu.make_async_remote_copy(
            src_ref=red_src.at[i],
            dst_ref=red_in.at[i],
            send_sem=red_send.at[i],
            recv_sem=red_recv.at[i],
            device_id=(me, peer),
            device_id_type=MESH,
        )
        copy.start()
        red_out.append(copy)
    total = share(head)
    for i in (2, 0, 1):
        red_out[i].wait_recv()
        total = total + red_in[i].astype(F32)
    out_ref[...] = total.astype(out_ref.dtype)
    for copy in (*qg_out, *bias_out, *st_out, *red_out):
        copy.wait_send()


def solution(mesh):
    nb = mesh.shape["blk"]

    def body(vertices, grad_out, w_query, w_key, w_value, w_out, pair_bins, bias_table, head_index):
        rows, width = vertices.shape
        feats = w_query.shape[1]
        pairs = feats // PAIR
        vmem, smem, dma = pltpu.VMEM, pltpu.SMEM, pltpu.SemaphoreType.DMA
        scratch = [
            vmem((rows, width), BF16),
            vmem((rows, width), BF16),
            vmem((width, feats), BF16),
            vmem((width, feats), BF16),
            vmem((width, feats), BF16),
            vmem((feats, width), BF16),
            smem(pair_bins.shape, jnp.int32),
            smem(bias_table.shape, F32),
            smem(head_index.shape, jnp.int32),
            vmem((WIDTH, 2, rows, feats), BF16),
            vmem((WIDTH, 2, rows, feats), BF16),
            vmem((WIDTH, pairs, 2 * rows, PAIR), BF16),
            vmem((WIDTH, pairs, 2 * rows, PAIR), BF16),
            vmem((WIDTH, pairs, rows, 2 * rows), F32),
            vmem((WIDTH, pairs, rows, 2 * rows), F32),
            vmem((WIDTH, pairs, rows, 2 * rows), F32),
            vmem((WIDTH, pairs, rows, 2 * rows), F32),
            vmem((WIDTH, pairs, rows // GROUP, 2 * rows), F32),
            vmem((WIDTH, pairs, rows // GROUP, 2 * rows), F32),
            vmem((4 * pairs, rows), F32),
            vmem((WIDTH, 4 * pairs, rows), F32),
            vmem((pairs, rows, PAIR), F32),
            vmem((pairs, rows, PAIR), F32),
            vmem((rows, width), F32),
            vmem((3, rows, feats), BF16),
            vmem((3, rows, feats), BF16),
            vmem((width // feats, 2 * feats, feats), BF16),
            dma((9,)),
            dma((4,)), dma((WIDTH,)),
            dma((4,)), dma((WIDTH,)),
            dma((4,)), dma((WIDTH,)),
            dma((4,)), dma((WIDTH,)),
            dma((3,)), dma((3,)),
        ]
        return pl.pallas_call(
            functools.partial(kernel, nb),
            out_shape=pltpu.VMEM((rows, feats), BF16),
            in_specs=[pl.BlockSpec(memory_space=pl.ANY)] * 9,
            out_specs=pl.BlockSpec(memory_space=pltpu.VMEM),
            scratch_shapes=scratch,
            compiler_params=pltpu.CompilerParams(
                collective_id=0, has_side_effects=True, vmem_limit_bytes=32 * 2**20
            ),
            name="attend_backward",
        )(*(pltpu.with_memory_space_constraint(a, pltpu.HBM) for a in (
            vertices, grad_out, w_query, w_key, w_value, w_out, pair_bins, bias_table, head_index
        )))

    in_specs = (
        P("blk", None),
        P("blk", None),
        P(None, "head"),
        P(None, "head"),
        P(None, "head"),
        P("head", None),
        P("blk", None),
        P(),
        P("head"),
    )
    return jax.shard_map(body, mesh=mesh, in_specs=in_specs, out_specs=P("blk", "head"), check_vma=False)
```

```python
import functools
import math

import jax
import jax.numpy as jnp
from jax import lax
from jax.experimental import pallas as pl
from jax.experimental.pallas import tpu as pltpu
from jax.sharding import PartitionSpec as P

HEAD_DIM = 64
REACH = 2
GROUP = 32
WIDTH = 2 * REACH + 1
PAIR = 2 * HEAD_DIM
LOG2E = math.log2(math.e)
MESH = pl.DeviceIdType.MESH
F32 = jnp.float32
BF16 = jnp.bfloat16


def dot_nn(a, b):
    return lax.dot_general(a, b, (((1,), (0,)), ((), ())), preferred_element_type=F32)


def dot_nt(a, b):
    return lax.dot_general(a, b, (((1,), (1,)), ((), ())), preferred_element_type=F32)


def kernel(
    nb,
    x_hbm, g_hbm, wq_hbm, wk_hbm, wv_hbm, wo_hbm, bins_hbm, table_hbm, hid_hbm,
    out_ref,
    x, g, wq, wk, wv, wo, bins, table, hid,
    kv, qg, qbd, gbd, ew, dp, s2, dp2, bias, bias_in, st_src, st_in, dk, dv, part, red_src, red_in, turned,
    in_sem, kv_send, kv_recv, qg_send, qg_recv, bias_send, bias_recv, st_send, st_recv, red_send, red_recv,
):
    rows = x.shape[0]
    feats = wq.shape[1]
    pairs = feats // PAIR
    groups = rows // GROUP
    me = lax.axis_index("blk")
    head = lax.axis_index("head")
    peers = (lax.rem(head + 2, 4), 3 - head, head + 1 - 2 * lax.rem(head, 2))

    def block(by):
        return lax.rem(me + (by + nb), nb)

    far = 2 * lax.rem(me, 2) - 1
    near = (far, -far, REACH, -REACH)
    barrier = pltpu.get_barrier_semaphore()
    for by in near:
        pl.semaphore_signal(barrier, inc=1, device_id=(block(by), head), device_id_type=MESH)
    for peer in peers:
        pl.semaphore_signal(barrier, inc=1, device_id=(me, peer), device_id_type=MESH)

    loads = [
        pltpu.make_async_copy(src, dst, in_sem.at[i])
        for i, (src, dst) in enumerate(
            (
                (x_hbm, x), (wk_hbm, wk), (wv_hbm, wv), (wq_hbm, wq), (g_hbm, g), (wo_hbm, wo),
                (bins_hbm, bins), (table_hbm, table), (hid_hbm, hid),
            )
        )
    ]
    for load in loads[:3]:
        load.start()

    def to_block(src, dst, send, recv, i):
        by = near[i]
        return pltpu.make_async_remote_copy(
            src_ref=src,
            dst_ref=dst.at[REACH - by],
            send_sem=send.at[i],
            recv_sem=recv.at[REACH - by],
            device_id=(block(by), head),
            device_id_type=MESH,
        )

    slots = (REACH, *(REACH - by for by in near))

    def wait_from(copies, tile):
        copies[tile - 1].wait_recv()

    loads[0].wait()
    loads[1].wait()
    for load in loads[3:]:
        load.start()
    kv[REACH, 0] = dot_nn(x[...], wk[...]).astype(BF16)
    loads[2].wait()
    kv[REACH, 1] = dot_nn(x[...], wv[...]).astype(BF16)
    pl.semaphore_wait(barrier, len(near) + len(peers))
    kv_out = [to_block(kv.at[REACH], kv, kv_send, kv_recv, i) for i in range(len(near))]
    for copy in kv_out:
        copy.start()
    loads[3].wait()
    qg[REACH, 0] = (dot_nn(x[...], wq[...]).astype(BF16).astype(F32) * (HEAD_DIM**-0.5)).astype(BF16)
    loads[4].wait()
    loads[5].wait()
    qg[REACH, 1] = dot_nt(g[...], wo[...]).astype(BF16)
    low_lane = lax.broadcasted_iota(jnp.int32, (rows, PAIR), 1) < HEAD_DIM
    zero = jnp.zeros((rows, PAIR), BF16)

    def spread(tile):
        for pr in range(pairs):
            cols = pl.ds(pr * PAIR, PAIR)
            for which, dst in ((0, qbd), (1, gbd)):
                both = qg[slots[tile], which, :, cols]
                dst[tile, pr, pl.ds(0, rows), :] = jnp.where(low_lane, both, zero)
                dst[tile, pr, pl.ds(rows, rows), :] = jnp.where(low_lane, zero, both)

    spread(0)

    loads[6].wait()
    loads[7].wait()
    loads[8].wait()
    lane_group = lax.broadcasted_iota(jnp.int32, (1, rows), 1) // GROUP

    def bias_rows(slot, carry):
        for h in range(2 * pairs):
            lines = []
            for kg in range(groups):
                line = jnp.zeros((1, rows), F32)
                for gr in range(groups):
                    line = jnp.where(lane_group == gr, table[hid[h], bins[gr, slot * groups + kg]], line)
                lines.append(line)
            bias[slot, h // 2, :, pl.ds((h % 2) * rows, rows)] = jnp.concatenate(lines, axis=0) * LOG2E
        return carry

    lax.fori_loop(0, WIDTH, bias_rows, 0)

    def grouped(tile):
        return tile.reshape(groups, GROUP, 2 * rows)

    stats = {}

    def key_tile(tile):
        slot = slots[tile]
        for pr in range(pairs):
            cols = pl.ds(pr * PAIR, PAIR)
            score = dot_nt(kv[slot, 0, :, cols], qbd[0, pr])
            weigh = dot_nt(kv[slot, 1, :, cols], gbd[0, pr])
            shift = bias[slot, pr]
            logit = grouped(score) * LOG2E + shift[:, None, :]
            peak = jnp.max(logit, axis=(0, 1), keepdims=True)
            expo = jnp.exp2(logit - peak).reshape(rows, 2 * rows)
            ew[tile, pr] = expo
            dp[tile, pr] = weigh
            total = jnp.sum(expo, axis=0, keepdims=True)
            cross = jnp.sum(expo * weigh, axis=0, keepdims=True)
            stats[tile, pr] = (peak.reshape(1, 2 * rows), total, cross)

    order = (0, 3, 4, 1, 2)
    key_tile(0)
    qg_out = [to_block(qg.at[REACH], qg, qg_send, qg_recv, i) for i in range(len(near))]
    bias_out = [to_block(bias.at[REACH + near[i]], bias_in, bias_send, bias_recv, i) for i in range(len(near))]
    for copy in kv_out:
        copy.wait_send()
    for copy in (*qg_out, *bias_out):
        copy.start()
    wait_from(kv_out, order[1])
    key_tile(order[1])
    wait_from(kv_out, order[2])
    key_tile(order[2])
    for j in range(x.shape[1] // feats):
        lines = pl.ds(j * feats, feats)
        turned[j, pl.ds(0, feats), :] = wk[lines, :].T
        turned[j, pl.ds(feats, feats), :] = wv[lines, :].T
    wait_from(kv_out, order[3])
    key_tile(order[3])
    early = []
    for pr in range(pairs):
        four = [stats[s, pr] for s in (0, 1, 3, 4)]
        top = functools.reduce(jnp.maximum, [f[0] for f in four])
        lift = [jnp.exp2(f[0] - top) for f in four]
        early.append(
            (top, sum(f[1] * up for f, up in zip(four, lift)), sum(f[2] * up for f, up in zip(four, lift)))
        )
    wait_from(kv_out, order[4])
    key_tile(order[4])

    scale = {}
    dots = []
    for pr in range(pairs):
        last = stats[2, pr]
        top = jnp.maximum(early[pr][0], last[0])
        up, down = jnp.exp2(early[pr][0] - top), jnp.exp2(last[0] - top)
        total = early[pr][1] * up + last[1] * down
        cross = early[pr][2] * up + last[2] * down
        inverse = 1.0 / total
        lse = top + jnp.log2(total)
        row_dot = cross * inverse
        dots.append(row_dot)
        for s in range(WIDTH):
            scale[s, pr] = jnp.exp2(stats[s, pr][0] - lse)
        for half in range(2):
            cols = slice(half * rows, (half + 1) * rows)
            st_src[pl.ds(2 * pr + half, 1), :] = lse[:, cols]
            st_src[pl.ds(2 * (pairs + pr) + half, 1), :] = row_dot[:, cols]
    st_out = [to_block(st_src, st_in, st_send, st_recv, i) for i in range(len(near))]
    for copy in st_out:
        copy.start()

    low_row = lax.broadcasted_iota(jnp.int32, (PAIR, rows), 0) < HEAD_DIM
    grad_query = []
    for pr in range(pairs):
        cols = pl.ds(pr * PAIR, PAIR)
        acc = jnp.zeros((PAIR, rows), F32)
        for tile in order:
            prob = ew[tile, pr] * scale[tile, pr]
            grad_score = (prob * (dp[tile, pr] - dots[pr])).astype(BF16)
            key_t = kv[slots[tile], 0, :, cols].astype(F32).T
            key_m = jnp.concatenate(
                [jnp.where(low_row, key_t, 0.0), jnp.where(low_row, 0.0, key_t)], axis=1
            ).astype(BF16)
            stacked = jnp.concatenate([grad_score[:, :rows], grad_score[:, rows:]], axis=0)
            acc = acc + dot_nn(key_m, stacked)
            if tile == 0:
                dk[pr] = dot_nn(grad_score, qbd[0, pr])
                dv[pr] = dot_nn(prob.astype(BF16), gbd[0, pr])
        grad_query.append((acc * (HEAD_DIM**-0.5)).T.astype(BF16))
    query_all = jnp.concatenate(grad_query, axis=1)
    part[...] = dot_nt(query_all, wq[...])

    others = (3, 4, 1, 2)
    for tile in others:
        slot = slots[tile]
        wait_from(qg_out, tile)
        wait_from(bias_out, tile)
        spread(tile)
        for pr in range(pairs):
            cols = pl.ds(pr * PAIR, PAIR)
            score = dot_nt(kv[REACH, 0, :, cols], qbd[tile, pr])
            s2[tile, pr] = (grouped(score) * LOG2E + bias_in[slot, pr][:, None, :]).reshape(rows, 2 * rows)
            dp2[tile, pr] = dot_nt(kv[REACH, 1, :, cols], gbd[tile, pr])

    def query_tile(tile):
        slot = slots[tile]
        for pr in range(pairs):
            lse, row_dot = (
                jnp.concatenate([st_in[slot, pl.ds(2 * at + half, 1), :] for half in range(2)], axis=1)
                for at in (pr, pairs + pr)
            )
            prob = jnp.exp2(s2[tile, pr] - lse)
            grad_score = (prob * (dp2[tile, pr] - row_dot)).astype(BF16)
            dk[pr] += dot_nn(grad_score, qbd[tile, pr])
            dv[pr] += dot_nn(prob.astype(BF16), gbd[tile, pr])

    wait_from(st_out, others[0])
    query_tile(others[0])
    wait_from(st_out, others[1])
    query_tile(others[1])
    wait_from(st_out, others[2])
    query_tile(others[2])
    wait_from(st_out, others[3])
    query_tile(others[3])
    key_all = jnp.concatenate([dk[pr].astype(BF16) for pr in range(pairs)], axis=1)
    value_all = jnp.concatenate([dv[pr].astype(BF16) for pr in range(pairs)], axis=1)

    both_all = jnp.concatenate([key_all, value_all], axis=1)

    def share(j):
        lines = pl.ds(pl.multiple_of(j * feats, feats), feats)
        return part[:, lines] + dot_nn(both_all, turned[j])

    red_out = []
    for i, peer in enumerate(peers):
        red_src[i] = share(peer).astype(BF16)
        copy = pltpu.make_async_remote_copy(
            src_ref=red_src.at[i],
            dst_ref=red_in.at[i],
            send_sem=red_send.at[i],
            recv_sem=red_recv.at[i],
            device_id=(me, peer),
            device_id_type=MESH,
        )
        copy.start()
        red_out.append(copy)
    total = share(head)
    for i in (2, 0, 1):
        red_out[i].wait_recv()
        total = total + red_in[i].astype(F32)
    out_ref[...] = total.astype(out_ref.dtype)
    for copy in (*qg_out, *bias_out, *st_out, *red_out):
        copy.wait_send()


def solution(mesh):
    nb = mesh.shape["blk"]

    def body(vertices, grad_out, w_query, w_key, w_value, w_out, pair_bins, bias_table, head_index):
        rows, width = vertices.shape
        feats = w_query.shape[1]
        pairs = feats // PAIR
        vmem, smem, dma = pltpu.VMEM, pltpu.SMEM, pltpu.SemaphoreType.DMA
        scratch = [
            vmem((rows, width), BF16),
            vmem((rows, width), BF16),
            vmem((width, feats), BF16),
            vmem((width, feats), BF16),
            vmem((width, feats), BF16),
            vmem((feats, width), BF16),
            smem(pair_bins.shape, jnp.int32),
            smem(bias_table.shape, F32),
            smem(head_index.shape, jnp.int32),
            vmem((WIDTH, 2, rows, feats), BF16),
            vmem((WIDTH, 2, rows, feats), BF16),
            vmem((WIDTH, pairs, 2 * rows, PAIR), BF16),
            vmem((WIDTH, pairs, 2 * rows, PAIR), BF16),
            vmem((WIDTH, pairs, rows, 2 * rows), F32),
            vmem((WIDTH, pairs, rows, 2 * rows), F32),
            vmem((WIDTH, pairs, rows, 2 * rows), F32),
            vmem((WIDTH, pairs, rows, 2 * rows), F32),
            vmem((WIDTH, pairs, rows // GROUP, 2 * rows), F32),
            vmem((WIDTH, pairs, rows // GROUP, 2 * rows), F32),
            vmem((4 * pairs, rows), F32),
            vmem((WIDTH, 4 * pairs, rows), F32),
            vmem((pairs, rows, PAIR), F32),
            vmem((pairs, rows, PAIR), F32),
            vmem((rows, width), F32),
            vmem((3, rows, feats), BF16),
            vmem((3, rows, feats), BF16),
            vmem((width // feats, 2 * feats, feats), BF16),
            dma((9,)),
            dma((4,)), dma((WIDTH,)),
            dma((4,)), dma((WIDTH,)),
            dma((4,)), dma((WIDTH,)),
            dma((4,)), dma((WIDTH,)),
            dma((3,)), dma((3,)),
        ]
        return pl.pallas_call(
            functools.partial(kernel, nb),
            out_shape=pltpu.VMEM((rows, feats), BF16),
            in_specs=[pl.BlockSpec(memory_space=pl.ANY)] * 9,
            out_specs=pl.BlockSpec(memory_space=pltpu.VMEM),
            scratch_shapes=scratch,
            compiler_params=pltpu.CompilerParams(
                collective_id=0, has_side_effects=True, vmem_limit_bytes=32 * 2**20
            ),
            name="attend_backward",
        )(*(pltpu.with_memory_space_constraint(a, pltpu.HBM) for a in (
            vertices, grad_out, w_query, w_key, w_value, w_out, pair_bins, bias_table, head_index
        )))

    in_specs = (
        P("blk", None),
        P("blk", None),
        P(None, "head"),
        P(None, "head"),
        P(None, "head"),
        P("head", None),
        P("blk", None),
        P(),
        P("head"),
    )
    return jax.shard_map(body, mesh=mesh, in_specs=in_specs, out_specs=P("blk", "head"), check_vma=False)
```
